256 devices in a mesh: chan: 128 (over x, y, z), tm: 2 (over core).
Axes of the slice: x: 4, y: 4, z: 8, core: 2. Of those that a mesh axis runs over, the one named last changes fastest.
Arguments:
- traces: bfloat16 [2, 128, 128, 1536], P('tm', 'chan'), may hold values from -2.5 to 2.5
- pair_target: int32 [128, 3], P('chan'), may hold values from 1 to 127, as said below
- pair_count: int32 [128], P('chan'), may hold values from 0 to 3, as said below
Outputs:
- stacked: float32 [128, 3, 33, 128, 128], P('chan', None, None, 'tm')
The draws below stay inside these ranges and needn't reach their ends.
Inputs may be any that keep to these rules, and one draw needn't show every extreme that they name: For j < pair_count[b], the entries pair_target[b, j] are distinct blocks among b + 1 .. b + 7; later slots hold arbitrary blocks above b, or b itself for the last block. pair_count[b] is at most the number of blocks after b; the last block has none.
All inputs are finite; a program needn't handle non-finite values.
Results may differ from the reference program's by a relative error of at most 0.0003.
Values may be sent and summed in bfloat16 or wider, within the bound.
No kernel may reach another device: no remote copies, remote signals or barrier semaphores. Data moves between devices by JAX's collectives and lax.ppermute only.
A program may use at most 128 MiB of HBM per device.

```python
import jax
import jax.numpy as jnp
from jax import lax

CH = 128
SAMP = 1536
MAXLAG = 16
REACH = 7
P_MAX = 3
BLOCKS = 128
SEGS = 2


def pair_lists(key):
    score_key = jax.random.fold_in(key, 11)
    count_key = jax.random.fold_in(key, 12)
    block_ids = jnp.arange(BLOCKS, dtype=jnp.int32)[:, None]
    offset_ids = jnp.arange(REACH, dtype=jnp.int32)[None, :]
    avail = jnp.minimum(REACH, BLOCKS - 1 - block_ids)
    scores = jax.random.randint(score_key, (BLOCKS, REACH), 0, 1 << 20) * 8 + offset_ids
    scores = scores + (offset_ids + 1 > avail).astype(jnp.int32) * (1 << 24)
    scores = scores - ((block_ids == 0) & (offset_ids == 0)).astype(jnp.int32) * (1 << 24)
    order = jnp.argsort(scores, axis=1, stable=True).astype(jnp.int32)
    offsets = order[:, :P_MAX] + 1
    targets = jnp.minimum(block_ids + offsets, BLOCKS - 1).astype(jnp.int32)
    counts = jax.random.randint(count_key, (BLOCKS,), 1, P_MAX + 1)
    counts = jnp.minimum(counts, avail[:, 0])
    counts = counts.at[0].set(P_MAX).astype(jnp.int32)
    return (targets, counts)


def draw_pair_target(key, part):
    return pair_lists(key)[0]


def draw_pair_count(key, part):
    return pair_lists(key)[1]


def block_scale(stream_key, shape, shards, least, largest):
    gain = 1.0
    for position, shards_of in shards:
        heights = jax.random.uniform(jax.random.fold_in(jax.random.fold_in(stream_key, 6), position), (shards_of,), jnp.float32, least / len(shards), largest / len(shards))
        gain = gain * jnp.repeat(jnp.exp(heights), shape[position] // shards_of).reshape((-1,) + (1,) * (len(shape) - 1 - position))
    return gain


def noise(own_key, dims, spread, most, shards=(), kind=jnp.bfloat16):
    drawn = jax.random.normal(own_key, dims, jnp.float32) * spread
    if len(shards) > 0:
        drawn = block_scale(own_key, dims, shards, -0.22, 0.18) * drawn
    return jnp.clip(drawn, min=-most, max=most).astype(kind)


def setup_inputs(seed: int = 0) -> dict:
    keys = jax.random.split(jax.random.key(seed), 4)
    traces = noise(keys[0], (SEGS, BLOCKS, CH, SAMP), (SAMP ** -0.25), 2.5, ((0, 2), (1, 128)))
    pair_target = draw_pair_target(jax.random.fold_in(keys[3], 71), 0)
    pair_count = draw_pair_count(jax.random.fold_in(keys[3], 71), 0)
    return dict(traces=traces, pair_target=pair_target, pair_count=pair_count)


def correlate(source, target):
    lag_total = 2 * MAXLAG + 1
    samples = source.shape[1]
    source = source.astype(jnp.float32)
    padded = jnp.pad(target.astype(jnp.float32), ((0, 0), (MAXLAG, MAXLAG)))
    pieces = []
    for lag_start in range(0, lag_total, 11):
        shifted = jnp.stack([padded[:, lag_index:lag_index + samples] for lag_index in range(lag_start, min(lag_start + 11, lag_total))])
        pieces.append(jnp.einsum("it,lkt->lik", source, shifted, precision=lax.Precision.HIGHEST))
    return jnp.concatenate(pieces, 0)


def reference(traces, pair_target, pair_count):
    def one_block(block_id):
        source_all = lax.dynamic_index_in_dim(traces, block_id, 1, keepdims=False)
        tiles = []
        for slot_id in range(P_MAX):
            target_id = pair_target[block_id, slot_id].astype(jnp.int32)
            target_all = lax.dynamic_index_in_dim(traces, target_id, 1, keepdims=False)
            total = correlate(source_all[0], target_all[0])
            for segment in range(1, SEGS):
                total = total + correlate(source_all[segment], target_all[segment])
            live = (slot_id < pair_count[block_id]).astype(jnp.float32)
            tiles.append(total * live)
        return jnp.stack(tiles)

    return lax.map(one_block, jnp.arange(BLOCKS, dtype=jnp.int32))
```

```python
import functools

import jax
import jax.numpy as jnp
from jax import lax
from jax.experimental import pallas as pl
from jax.experimental.pallas import tpu as pltpu
from jax.sharding import PartitionSpec as P

MAXLAG = 16
REACH = 7
P_MAX = 3
LAGS = 2 * MAXLAG + 1
PAIRS = MAXLAG + 1
EDGE = 128
VMEM = pl.BlockSpec(memory_space=pltpu.VMEM)
SMEM = pl.BlockSpec(memory_space=pltpu.SMEM)
ANY = pl.BlockSpec(memory_space=pl.ANY)
CHUNKS = ((0, 4), (4, 8), (8, 12), (12, 17))


def stack_kernel(first, second, out, padded):
    half, samples = first.shape
    padded[...] = jnp.zeros_like(padded)
    for g, source in enumerate((first, second)):
        padded[:, EDGE : EDGE + samples] = source[...]
        for m in range(PAIRS):
            start = EDGE + MAXLAG - 2 * m
            out[m * half : (m + 1) * half, g * samples : (g + 1) * samples] = padded[:, start : start + samples]
    lane = lax.broadcasted_iota(jnp.int32, (half, EDGE), 1)
    for m in range(PAIRS):
        at = MAXLAG - 1 - 2 * m
        edge = jnp.zeros((half, EDGE), jnp.float32)
        if at >= 0:
            for g, source in enumerate((first, second)):
                column = source[:, :EDGE].astype(jnp.float32)[:, at : at + 1]
                edge = jnp.where(lane == g, column, edge)
        out[m * half : (m + 1) * half, 2 * samples :] = edge.astype(jnp.bfloat16)


def stack(first, second):
    half, samples = first.shape
    return pl.pallas_call(
        stack_kernel,
        out_shape=jax.ShapeDtypeStruct((PAIRS * half, 2 * samples + EDGE), jnp.bfloat16),
        in_specs=[VMEM, VMEM],
        out_specs=VMEM,
        scratch_shapes=[pltpu.VMEM((half, samples + 2 * EDGE), jnp.bfloat16)],
        compiler_params=pltpu.CompilerParams(vmem_limit_bytes=24 * 2**20),
        name="stack",
    )(first, second)


def fill_columns(own, other, columns):
    count, samples = own.shape
    lane = lax.broadcasted_iota(jnp.int32, (count, EDGE), 1)
    edge = jnp.zeros((count, EDGE), jnp.float32)
    for g, target in enumerate((own, other)):
        block = target[...]
        columns[:count, g * samples : (g + 1) * samples] = block
        ahead = jnp.concatenate([block[:, 1:], jnp.zeros((count, 1), block.dtype)], 1)
        columns[count:, g * samples : (g + 1) * samples] = ahead
        edge = jnp.where(lane == g, block[:, :EDGE].astype(jnp.float32)[:, :1], edge)
    columns[:count, 2 * samples :] = jnp.zeros((count, EDGE), jnp.bfloat16)
    columns[count:, 2 * samples :] = edge.astype(jnp.bfloat16)


def tile_kernel(distances, first, *refs):
    n = len(distances)
    wanted, stacked = refs[0], refs[1]
    own, other = refs[2 : 2 + n], refs[2 + n : 2 + 2 * n]
    out, columns, rows, tile, row_sem, out_sem = refs[-6:]
    count = own[0].shape[0]
    half = rows.shape[0] // PAIRS

    def is_here(slot):
        here = wanted[slot] == distances[0]
        for d in distances[1:]:
            here = jnp.logical_or(here, wanted[slot] == d)
        return here

    some = jnp.logical_or(jnp.logical_or(is_here(0), is_here(1)), is_here(2))
    row_copy = pltpu.make_async_copy(stacked, rows, row_sem)

    @pl.when(some)
    def _():
        row_copy.start()

    def send(slot, c):
        low, high = CHUNKS[c]
        lags = pl.ds(2 * low, min(2 * high, LAGS) - 2 * low)
        return pltpu.make_async_copy(tile.at[lags], out.at[0, slot, lags], out_sem.at[c])

    if first:

        @pl.loop(0, P_MAX)
        def _(slot):
            @pl.when(wanted[slot] == 0)
            def _():
                tile[...] = jnp.zeros_like(tile)
                for c in range(len(CHUNKS)):
                    send(slot, c).start()
                for c in range(len(CHUNKS)):
                    send(slot, c).wait()

    @pl.when(some)
    def _():
        row_copy.wait()

    @pl.loop(0, P_MAX)
    def _(slot):
        @pl.when(is_here(slot))
        def _():
            for k, d in enumerate(distances):

                @pl.when(wanted[slot] == d)
                def _(k=k):
                    fill_columns(own[k], other[k], columns)

            for c, (low, high) in enumerate(CHUNKS):
                got = lax.dot_general(
                    rows[low * half : high * half, :],
                    columns[...],
                    (((1,), (1,)), ((), ())),
                    preferred_element_type=jnp.float32,
                )
                for m in range(low, high):
                    part = got[(m - low) * half : (m - low + 1) * half]
                    tile[2 * m] = part[:, :count]
                    if 2 * m + 1 < LAGS:
                        tile[2 * m + 1] = part[:, count:]
                send(slot, c).start()
            for c in range(len(CHUNKS)):
                send(slot, c).wait()


def tiles(distances, wanted, stacked, own, other, so_far=None):
    rows = stacked.shape
    count, samples = own[0].shape
    half = rows[0] // PAIRS
    arguments = [wanted, stacked, *own, *other]
    specs = [SMEM, ANY] + [VMEM] * (2 * len(own))
    aliases = {}
    if so_far is not None:
        aliases = {len(arguments): 0}
        arguments.append(so_far)
        specs.append(ANY)
    return pl.pallas_call(
        functools.partial(tile_kernel, distances, so_far is None),
        out_shape=jax.ShapeDtypeStruct((1, P_MAX, LAGS, half, count), jnp.float32),
        in_specs=specs,
        out_specs=ANY,
        scratch_shapes=[
            pltpu.VMEM((2 * count, rows[1]), jnp.bfloat16),
            pltpu.VMEM(rows, jnp.bfloat16),
            pltpu.VMEM((LAGS, half, count), jnp.float32),
            pltpu.SemaphoreType.DMA,
            pltpu.SemaphoreType.DMA((len(CHUNKS),)),
        ],
        input_output_aliases=aliases,
        compiler_params=pltpu.CompilerParams(vmem_limit_bytes=24 * 2**20),
        name="tiles_" + "_".join(map(str, distances)),
    )(*arguments)


def body(traces, pair_target, pair_count):
    own = traces[0, 0]
    half = own.shape[0] // 2
    blocks = lax.axis_size("chan")
    me, core = lax.axis_index("chan"), lax.axis_index("tm")
    slots = jnp.arange(P_MAX, dtype=jnp.int32)
    wanted = jnp.where(slots < pair_count[0], pair_target[0] - me, 0).astype(jnp.int32)

    row = 8
    everyone = range(blocks)
    down = [((i + 1) % blocks, i) for i in everyone]
    up = [((i - 1) % blocks, i) for i in everyone]
    next_row = [((i + row) % blocks, i) if i % row < row - 1 else (i, i) for i in everyone]
    turn = [(i - 1, i) if i % row else (i + row - 1, i) for i in everyone]

    def move(block, route):
        return lax.ppermute(block, "chan", route)

    def swap(block):
        return lax.ppermute(block, "tm", [(0, 1), (1, 0)])

    below = move(own, next_row)
    d1 = move(own, down)
    d7 = move(below, turn)
    d2 = move(d1, down)
    d6 = move(d7, up)
    d3 = move(d2, down)
    d5 = move(d6, up)
    d4 = move(d3, down)

    mine = lax.dynamic_slice_in_dim(own, core * half, half, 0)
    theirs = swap(lax.dynamic_slice_in_dim(own, (1 - core) * half, half, 0))
    rows = stack(mine, theirs)
    result = None
    for distances, held in (((1, 7), (d1, d7)), ((2, 6), (d2, d6)), ((3, 5), (d3, d5)), ((4,), (d4,))):
        result = tiles(distances, wanted, rows, held, [swap(b) for b in held], result)
    return result


def solution(mesh):
    placed = (P("tm", "chan", None, None), P("chan", None), P("chan"))
    return jax.shard_map(
        body,
        mesh=mesh,
        in_specs=placed,
        out_specs=P("chan", None, None, "tm", None),
        check_vma=False,
    )
```

```python
import functools

import jax
import jax.numpy as jnp
from jax import lax
from jax.experimental import pallas as pl
from jax.experimental.pallas import tpu as pltpu
from jax.sharding import PartitionSpec as P

MAXLAG = 16
REACH = 7
P_MAX = 3
LAGS = 2 * MAXLAG + 1
PAIRS = MAXLAG + 1
EDGE = 128
FREE = pl.CostEstimate(flops=0, bytes_accessed=0, transcendentals=0)
VMEM = pl.BlockSpec(memory_space=pltpu.VMEM)
SMEM = pl.BlockSpec(memory_space=pltpu.SMEM)
ANY = pl.BlockSpec(memory_space=pl.ANY)


def stack_kernel(wanted, first, second, out, result, padded, empty, sem):
    half, samples = first.shape
    empty[...] = jnp.zeros_like(empty)
    for action in ("start", "wait"):
        for slot in range(P_MAX):

            @pl.when(wanted[slot] == 0)
            def _(slot=slot):
                copy = pltpu.make_async_copy(empty, result.at[0, slot], sem)
                copy.start() if action == "start" else copy.wait()

        if action == "wait":
            return
        padded[...] = jnp.zeros_like(padded)
        for g, source in enumerate((first, second)):
            padded[:, EDGE : EDGE + samples] = source[...]
            for m in range(PAIRS):
                start = EDGE + MAXLAG - 2 * m
                out[m * half : (m + 1) * half, g * samples : (g + 1) * samples] = padded[:, start : start + samples]
        lane = lax.broadcasted_iota(jnp.int32, (half, EDGE), 1)
        for m in range(PAIRS):
            at = MAXLAG - 1 - 2 * m
            edge = jnp.zeros((half, EDGE), jnp.float32)
            if at >= 0:
                for g, source in enumerate((first, second)):
                    column = source[:, :EDGE].astype(jnp.float32)[:, at : at + 1]
                    edge = jnp.where(lane == g, column, edge)
            out[m * half : (m + 1) * half, 2 * samples :] = edge.astype(jnp.bfloat16)


def stack(wanted, first, second):
    half, samples = first.shape
    return pl.pallas_call(
        stack_kernel,
        out_shape=[
            pltpu.VMEM((PAIRS * half, 2 * samples + EDGE), jnp.bfloat16),
            jax.ShapeDtypeStruct((1, P_MAX, LAGS, half, 2 * half), jnp.float32),
        ],
        in_specs=[SMEM, VMEM, VMEM],
        out_specs=[VMEM, ANY],
        scratch_shapes=[
            pltpu.VMEM((half, samples + 2 * EDGE), jnp.bfloat16),
            pltpu.VMEM((LAGS, half, 2 * half), jnp.float32),
            pltpu.SemaphoreType.DMA,
        ],
        compiler_params=pltpu.CompilerParams(vmem_limit_bytes=24 * 2**20),
        cost_estimate=FREE,
        name="stack",
    )(wanted, first, second)


def fill_columns(own, other, columns):
    count = columns.shape[0] // 2
    at = 0
    for pair in zip(own, other):
        size, samples = pair[0].shape
        low, high = pl.ds(at, size), pl.ds(count + at, size)
        lane = lax.broadcasted_iota(jnp.int32, (size, EDGE), 1)
        edge = jnp.zeros((size, EDGE), jnp.float32)
        for g, target in enumerate(pair):
            block = target[...]
            columns[low, g * samples : (g + 1) * samples] = block
            ahead = jnp.concatenate([block[:, 1:], jnp.zeros((size, 1), block.dtype)], 1)
            columns[high, g * samples : (g + 1) * samples] = ahead
            edge = jnp.where(lane == g, block[:, :EDGE].astype(jnp.float32)[:, :1], edge)
        columns[low, 2 * samples :] = jnp.zeros((size, EDGE), jnp.bfloat16)
        columns[high, 2 * samples :] = edge.astype(jnp.bfloat16)
        at += size


def is_in(distance, distances):
    found = distance == distances[0]
    for d in distances[1:]:
        found = jnp.logical_or(found, distance == d)
    return found


def pick_kernel(distances, counts, wanted, *refs):
    n = sum(counts)
    parts, outs, sem = list(refs[:n]), refs[n:-1], refs[-1]
    blocks = [[parts.pop(0) for _ in range(c)] for c in counts]

    for action in ("start", "wait"):
        for slot in range(P_MAX):
            for d, block in zip(distances, blocks):

                @pl.when(wanted[slot] == d)
                def _(slot=slot, block=block):
                    size = block[0].shape[0]
                    for h, part in enumerate(block):
                        copy = pltpu.make_async_copy(part, outs[slot].at[pl.ds(h * size, size)], sem)
                        copy.start() if action == "start" else copy.wait()


def pick(distances, wanted, blocks):
    counts = [len(block) for block in blocks]
    size, samples = blocks[0][0].shape
    shape = jax.ShapeDtypeStruct((size * counts[0], samples), jnp.bfloat16)
    parts = [part for block in blocks for part in block]
    picked = pl.pallas_call(
        functools.partial(pick_kernel, distances, counts),
        out_shape=[shape] * P_MAX,
        in_specs=[SMEM] + [ANY] * len(parts),
        out_specs=[ANY] * P_MAX,
        scratch_shapes=[pltpu.SemaphoreType.DMA],
        compiler_params=pltpu.CompilerParams(vmem_limit_bytes=8 * 2**20),
        cost_estimate=FREE,
        name="pick",
    )(wanted, *parts)
    return list(picked)


def tile_kernel(distances, wanted, rows, *refs):
    own, other = refs[:P_MAX], refs[P_MAX : 2 * P_MAX]
    out, columns, tile, sem = refs[-4:]
    count = columns.shape[0] // 2
    half = rows.shape[0] // PAIRS

    @pl.loop(0, P_MAX)
    def _(slot):
        @pl.when(is_in(wanted[slot], distances))
        def _():
            for k in range(P_MAX):

                @pl.when(slot == k)
                def _(k=k):
                    fill_columns(own[k : k + 1], other[k : k + 1], columns)

            got = lax.dot_general(
                rows[...], columns[...], (((1,), (1,)), ((), ())), preferred_element_type=jnp.float32
            )
            for m in range(PAIRS):
                part = got[m * half : (m + 1) * half]
                tile[2 * m] = part[:, :count]
                if 2 * m + 1 < LAGS:
                    tile[2 * m + 1] = part[:, count:]
            copy = pltpu.make_async_copy(tile, out.at[0, slot], sem)
            copy.start()
            copy.wait()


def tiles(distances, wanted, stacked, own, other, so_far):
    rows = stacked.shape
    half = rows[0] // PAIRS
    count = 2 * half
    stacked = pltpu.with_memory_space_constraint(stacked, pltpu.VMEM)
    arguments = [wanted, stacked, *own, *other, so_far]
    return pl.pallas_call(
        functools.partial(tile_kernel, distances),
        out_shape=jax.ShapeDtypeStruct(so_far.shape, so_far.dtype),
        in_specs=[SMEM] + [VMEM] * (len(arguments) - 2) + [ANY],
        out_specs=ANY,
        scratch_shapes=[
            pltpu.VMEM((2 * count, rows[1]), jnp.bfloat16),
            pltpu.VMEM((LAGS, half, count), jnp.float32),
            pltpu.SemaphoreType.DMA,
        ],
        input_output_aliases={len(arguments) - 1: 0},
        compiler_params=pltpu.CompilerParams(vmem_limit_bytes=16 * 2**20),
        cost_estimate=FREE,
        name="tiles_" + "_".join(map(str, distances)),
    )(*arguments)


def body(traces, pair_target, pair_count):
    own = traces[0, 0]
    half = own.shape[0] // 2
    blocks = lax.axis_size("chan")
    me, core = lax.axis_index("chan"), lax.axis_index("tm")
    slots = jnp.arange(P_MAX, dtype=jnp.int32)
    wanted = jnp.where(slots < pair_count[0], pair_target[0] - me, 0).astype(jnp.int32)

    row = 8
    everyone = range(blocks)
    down = [((i + 1) % blocks, i) for i in everyone]
    up = [((i - 1) % blocks, i) for i in everyone]
    next_row = [((i + row) % blocks, i) if i % row < row - 1 else (i, i) for i in everyone]
    turn = [(i - 1, i) if i % row else (i + row - 1, i) for i in everyone]

    def move(parts, route):
        return [lax.ppermute(p, "chan", route) for p in parts]

    def swap(parts):
        return [lax.ppermute(p, "tm", [(0, 1), (1, 0)]) for p in parts]

    def step(*values):
        return lax.optimization_barrier(values)

    mine = lax.dynamic_slice_in_dim(own, core * half, half, 0)
    theirs = lax.dynamic_slice_in_dim(own, (1 - core) * half, half, 0)
    d1 = move([own], down)
    below = move([own], next_row)
    theirs = swap([theirs])[0]
    rows, result = stack(wanted, mine, theirs)
    below, rows, result = step(below, rows, result)
    d7 = move(below, turn)
    d2 = move(d1, down)
    d6 = move(d7, up)
    d3 = move(d2, down)
    d5 = move(d6, up)
    d4 = move(d3, down)
    near = pick((1, 7, 2, 6), wanted, [d1, d7, d2, d6])
    result = tiles((1, 7, 2, 6), wanted, rows, near, swap(near), result)
    d3, d5, d4, result = step(d3, d5, d4, result)
    far = pick((3, 5, 4), wanted, [d3, d5, d4])
    return tiles((3, 5, 4), wanted, rows, far, swap(far), result)


def solution(mesh):
    placed = (P("tm", "chan", None, None), P("chan", None), P("chan"))
    return jax.shard_map(
        body,
        mesh=mesh,
        in_specs=placed,
        out_specs=P("chan", None, None, "tm", None),
        check_vma=False,
    )
```

```python
import functools

import jax
import jax.numpy as jnp
from jax import lax
from jax.experimental import pallas as pl
from jax.experimental.pallas import tpu as pltpu
from jax.sharding import PartitionSpec as P

MAXLAG = 16
REACH = 7
P_MAX = 3
LAGS = 2 * MAXLAG + 1
PAIRS = MAXLAG + 1
EDGE = 128
FREE = pl.CostEstimate(flops=0, bytes_accessed=0, transcendentals=0)
VMEM = pl.BlockSpec(memory_space=pltpu.VMEM)
SMEM = pl.BlockSpec(memory_space=pltpu.SMEM)
ANY = pl.BlockSpec(memory_space=pl.ANY)


def stack_kernel(wanted, first, second, out, result, padded, empty, sem):
    half, samples = first.shape
    empty[...] = jnp.zeros_like(empty)
    for action in ("start", "wait"):
        for slot in range(P_MAX):

            @pl.when(wanted[slot] == 0)
            def _(slot=slot):
                copy = pltpu.make_async_copy(empty, result.at[0, slot], sem)
                copy.start() if action == "start" else copy.wait()

        if action == "wait":
            return
        padded[...] = jnp.zeros_like(padded)
        for g, source in enumerate((first, second)):
            padded[:, EDGE : EDGE + samples] = source[...]
            for m in range(PAIRS):
                start = EDGE + MAXLAG - 2 * m
                out[m * half : (m + 1) * half, g * samples : (g + 1) * samples] = padded[:, start : start + samples]
        lane = lax.broadcasted_iota(jnp.int32, (half, EDGE), 1)
        for m in range(PAIRS):
            at = MAXLAG - 1 - 2 * m
            edge = jnp.zeros((half, EDGE), jnp.float32)
            if at >= 0:
                for g, source in enumerate((first, second)):
                    column = source[:, :EDGE].astype(jnp.float32)[:, at : at + 1]
                    edge = jnp.where(lane == g, column, edge)
            out[m * half : (m + 1) * half, 2 * samples :] = edge.astype(jnp.bfloat16)


def stack(wanted, first, second):
    half, samples = first.shape
    return pl.pallas_call(
        stack_kernel,
        out_shape=[
            pltpu.VMEM((PAIRS * half, 2 * samples + EDGE), jnp.bfloat16),
            jax.ShapeDtypeStruct((1, P_MAX, LAGS, half, 2 * half), jnp.float32),
        ],
        in_specs=[SMEM, VMEM, VMEM],
        out_specs=[VMEM, ANY],
        scratch_shapes=[
            pltpu.VMEM((half, samples + 2 * EDGE), jnp.bfloat16),
            pltpu.VMEM((LAGS, half, 2 * half), jnp.float32),
            pltpu.SemaphoreType.DMA,
        ],
        compiler_params=pltpu.CompilerParams(vmem_limit_bytes=24 * 2**20),
        cost_estimate=FREE,
        name="stack",
    )(wanted, first, second)


def fill_columns(own, other, columns):
    count, samples = own.shape
    lane = lax.broadcasted_iota(jnp.int32, (count, EDGE), 1)
    edge = jnp.zeros((count, EDGE), jnp.float32)
    for g, target in enumerate((own, other)):
        block = target[...]
        columns[:count, g * samples : (g + 1) * samples] = block
        ahead = jnp.concatenate([block[:, 1:], jnp.zeros((count, 1), block.dtype)], 1)
        columns[count:, g * samples : (g + 1) * samples] = ahead
        edge = jnp.where(lane == g, block[:, :EDGE].astype(jnp.float32)[:, :1], edge)
    columns[:count, 2 * samples :] = jnp.zeros((count, EDGE), jnp.bfloat16)
    columns[count:, 2 * samples :] = edge.astype(jnp.bfloat16)


def is_in(distance, distances):
    found = distance == distances[0]
    for d in distances[1:]:
        found = jnp.logical_or(found, distance == d)
    return found


def pick_kernel(distances, wanted, *refs):
    n = len(distances)
    blocks, outs, sem = refs[:n], refs[n:-1], refs[-1]

    for action in ("start", "wait"):
        for slot in range(P_MAX):
            for d, block in zip(distances, blocks):

                @pl.when(wanted[slot] == d)
                def _(slot=slot, block=block):
                    copy = pltpu.make_async_copy(block, outs[slot], sem)
                    copy.start() if action == "start" else copy.wait()


def pick(distances, wanted, blocks):
    shape = jax.ShapeDtypeStruct(blocks[0].shape, jnp.bfloat16)
    picked = pl.pallas_call(
        functools.partial(pick_kernel, distances),
        out_shape=[shape] * P_MAX,
        in_specs=[SMEM] + [ANY] * len(blocks),
        out_specs=[ANY] * P_MAX,
        scratch_shapes=[pltpu.SemaphoreType.DMA],
        compiler_params=pltpu.CompilerParams(vmem_limit_bytes=8 * 2**20),
        cost_estimate=FREE,
        name="pick",
    )(wanted, *blocks)
    return list(picked)


def tile_kernel(distances, by_slot, wanted, rows, *refs):
    n = P_MAX if by_slot else len(distances)
    own, other = refs[:n], refs[n : 2 * n]
    out, columns, tile, sem = refs[-4:]
    count = columns.shape[0] // 2
    half = rows.shape[0] // PAIRS

    def send(slot):
        return pltpu.make_async_copy(tile.at[slot], out.at[0, slot], sem.at[slot])

    @pl.loop(0, P_MAX)
    def _(slot):
        @pl.when(is_in(wanted[slot], distances))
        def _():
            for k in range(n):

                @pl.when(slot == k if by_slot else wanted[slot] == distances[k])
                def _(k=k):
                    fill_columns(own[k], other[k], columns)

            got = lax.dot_general(
                rows[...], columns[...], (((1,), (1,)), ((), ())), preferred_element_type=jnp.float32
            )
            for m in range(PAIRS):
                part = got[m * half : (m + 1) * half]
                tile[slot, 2 * m] = part[:, :count]
                if 2 * m + 1 < LAGS:
                    tile[slot, 2 * m + 1] = part[:, count:]
            send(slot).start()

    @pl.loop(0, P_MAX)
    def _(slot):
        @pl.when(is_in(wanted[slot], distances))
        def _():
            send(slot).wait()


def tiles(distances, wanted, stacked, own, other, so_far, by_slot=False):
    rows = stacked.shape
    half = rows[0] // PAIRS
    count = 2 * half
    stacked = pltpu.with_memory_space_constraint(stacked, pltpu.VMEM)
    arguments = [wanted, stacked, *own, *other, so_far]
    return pl.pallas_call(
        functools.partial(tile_kernel, distances, by_slot),
        out_shape=jax.ShapeDtypeStruct(so_far.shape, so_far.dtype),
        in_specs=[SMEM] + [VMEM] * (len(arguments) - 2) + [ANY],
        out_specs=ANY,
        scratch_shapes=[
            pltpu.VMEM((2 * count, rows[1]), jnp.bfloat16),
            pltpu.VMEM((P_MAX, LAGS, half, count), jnp.float32),
            pltpu.SemaphoreType.DMA((P_MAX,)),
        ],
        input_output_aliases={len(arguments) - 1: 0},
        compiler_params=pltpu.CompilerParams(vmem_limit_bytes=16 * 2**20),
        cost_estimate=FREE,
        name="tiles_" + "_".join(map(str, distances)),
    )(*arguments)


def body(traces, pair_target, pair_count):
    own = traces[0, 0]
    half = own.shape[0] // 2
    blocks = lax.axis_size("chan")
    me, core = lax.axis_index("chan"), lax.axis_index("tm")
    slots = jnp.arange(P_MAX, dtype=jnp.int32)
    wanted = jnp.where(slots < pair_count[0], pair_target[0] - me, 0).astype(jnp.int32)

    row = 8
    everyone = range(blocks)
    down = [((i + 1) % blocks, i) for i in everyone]
    up = [((i - 1) % blocks, i) for i in everyone]
    next_row = [((i + row) % blocks, i) if i % row < row - 1 else (i, i) for i in everyone]
    turn = [(i - 1, i) if i % row else (i + row - 1, i) for i in everyone]

    def move(parts, route):
        return [lax.ppermute(p, "chan", route) for p in parts]

    def swap(parts):
        return [lax.ppermute(p, "tm", [(0, 1), (1, 0)]) for p in parts]

    def step(*values):
        return lax.optimization_barrier(values)

    mine = lax.dynamic_slice_in_dim(own, core * half, half, 0)
    theirs = lax.dynamic_slice_in_dim(own, (1 - core) * half, half, 0)
    d1 = move([own], down)[0]
    below = move([own], next_row)[0]
    before = move([own], turn)[0]
    theirs = swap([theirs])[0]
    below, before, theirs = step(below, before, theirs)
    d7 = move([below], turn)[0]
    d2 = move([d1], down[:-1])[0]
    rows, result = stack(wanted, mine, theirs)
    d7, rows, result = step(d7, rows, result)
    d6 = move([jnp.where(me % row == row - 1, before, d7)], turn)[0]
    d3 = move([d2], down)[0]
    d5 = move([d6], up)[0]
    d4 = move([d3], down)[0]
    near = pick((1, 7, 2, 6), wanted, [d1, d7, d2, d6])
    result = tiles((1, 7, 2, 6), wanted, rows, near, swap(near), result, True)
    d3, d5, result = step(d3, d5, result)
    return tiles((3, 5, 4), wanted, rows, [d3, d5, d4], swap([d3, d5, d4]), result)


def solution(mesh):
    placed = (P("tm", "chan", None, None), P("chan", None), P("chan"))
    return jax.shard_map(
        body,
        mesh=mesh,
        in_specs=placed,
        out_specs=P("chan", None, None, "tm", None),
        check_vma=False,
    )
```

```python
import functools

import jax
import jax.numpy as jnp
from jax import lax
from jax.experimental import pallas as pl
from jax.experimental.pallas import tpu as pltpu
from jax.sharding import PartitionSpec as P

MAXLAG = 16
REACH = 7
P_MAX = 3
LAGS = 2 * MAXLAG + 1
PAIRS = MAXLAG + 1
EDGE = 128
FREE = pl.CostEstimate(flops=0, bytes_accessed=0, transcendentals=0)
VMEM = pl.BlockSpec(memory_space=pltpu.VMEM)
SMEM = pl.BlockSpec(memory_space=pltpu.SMEM)
ANY = pl.BlockSpec(memory_space=pl.ANY)


def stack_kernel(wanted, first, second, out, result, padded, empty, sem):
    half, samples = first.shape
    empty[...] = jnp.zeros_like(empty)
    for action in ("start", "wait"):
        for slot in range(P_MAX):

            @pl.when(wanted[slot] == 0)
            def _(slot=slot):
                copy = pltpu.make_async_copy(empty, result.at[0, slot], sem)
                copy.start() if action == "start" else copy.wait()

        if action == "wait":
            return
        padded[...] = jnp.zeros_like(padded)
        for g, source in enumerate((first, second)):
            padded[:, EDGE : EDGE + samples] = source[...]
            for m in range(PAIRS):
                start = EDGE + MAXLAG - 2 * m
                out[m * half : (m + 1) * half, g * samples : (g + 1) * samples] = padded[:, start : start + samples]
        lane = lax.broadcasted_iota(jnp.int32, (half, EDGE), 1)
        for m in range(PAIRS):
            at = MAXLAG - 1 - 2 * m
            edge = jnp.zeros((half, EDGE), jnp.float32)
            if at >= 0:
                for g, source in enumerate((first, second)):
                    column = source[:, :EDGE].astype(jnp.float32)[:, at : at + 1]
                    edge = jnp.where(lane == g, column, edge)
            out[m * half : (m + 1) * half, 2 * samples :] = edge.astype(jnp.bfloat16)


def stack(wanted, first, second):
    half, samples = first.shape
    return pl.pallas_call(
        stack_kernel,
        out_shape=[
            pltpu.VMEM((PAIRS * half, 2 * samples + EDGE), jnp.bfloat16),
            jax.ShapeDtypeStruct((1, P_MAX, LAGS, half, 2 * half), jnp.float32),
        ],
        in_specs=[SMEM, VMEM, VMEM],
        out_specs=[VMEM, ANY],
        scratch_shapes=[
            pltpu.VMEM((half, samples + 2 * EDGE), jnp.bfloat16),
            pltpu.VMEM((LAGS, half, 2 * half), jnp.float32),
            pltpu.SemaphoreType.DMA,
        ],
        compiler_params=pltpu.CompilerParams(vmem_limit_bytes=24 * 2**20),
        cost_estimate=FREE,
        name="stack",
    )(wanted, first, second)


def fill_columns(own, other, columns):
    count, samples = own.shape
    lane = lax.broadcasted_iota(jnp.int32, (count, EDGE), 1)
    edge = jnp.zeros((count, EDGE), jnp.float32)
    for g, target in enumerate((own, other)):
        block = target[...]
        columns[:count, g * samples : (g + 1) * samples] = block
        ahead = jnp.concatenate([block[:, 1:], jnp.zeros((count, 1), block.dtype)], 1)
        columns[count:, g * samples : (g + 1) * samples] = ahead
        edge = jnp.where(lane == g, block[:, :EDGE].astype(jnp.float32)[:, :1], edge)
    columns[:count, 2 * samples :] = jnp.zeros((count, EDGE), jnp.bfloat16)
    columns[count:, 2 * samples :] = edge.astype(jnp.bfloat16)


def is_in(distance, distances):
    found = distance == distances[0]
    for d in distances[1:]:
        found = jnp.logical_or(found, distance == d)
    return found


def pick_kernel(distances, wanted, *refs):
    n = len(distances)
    blocks, outs, sem = refs[:n], refs[n:-1], refs[-1]

    for action in ("start", "wait"):
        for slot in range(P_MAX):
            for d, block in zip(distances, blocks):

                @pl.when(wanted[slot] == d)
                def _(slot=slot, block=block):
                    copy = pltpu.make_async_copy(block, outs[slot], sem)
                    copy.start() if action == "start" else copy.wait()


def pick(distances, wanted, blocks):
    shape = jax.ShapeDtypeStruct(blocks[0].shape, jnp.bfloat16)
    picked = pl.pallas_call(
        functools.partial(pick_kernel, distances),
        out_shape=[shape] * P_MAX,
        in_specs=[SMEM] + [ANY] * len(blocks),
        out_specs=[ANY] * P_MAX,
        scratch_shapes=[pltpu.SemaphoreType.DMA],
        compiler_params=pltpu.CompilerParams(vmem_limit_bytes=8 * 2**20),
        cost_estimate=FREE,
        name="pick",
    )(wanted, *blocks)
    return list(picked)


def tile_kernel(distances, by_slot, wanted, rows, *refs):
    n = P_MAX if by_slot else len(distances)
    own, other = refs[:n], refs[n : 2 * n]
    out, columns, tile, sem = refs[-4:]
    count = columns.shape[0] // 2
    half = rows.shape[0] // PAIRS

    def send(slot):
        return pltpu.make_async_copy(tile.at[slot], out.at[0, slot], sem.at[slot])

    @pl.loop(0, P_MAX)
    def _(slot):
        @pl.when(is_in(wanted[slot], distances))
        def _():
            for k in range(n):

                @pl.when(slot == k if by_slot else wanted[slot] == distances[k])
                def _(k=k):
                    fill_columns(own[k], other[k], columns)

            got = lax.dot_general(
                rows[...], columns[...], (((1,), (1,)), ((), ())), preferred_element_type=jnp.float32
            )
            for m in range(PAIRS):
                part = got[m * half : (m + 1) * half]
                tile[slot, 2 * m] = part[:, :count]
                if 2 * m + 1 < LAGS:
                    tile[slot, 2 * m + 1] = part[:, count:]
            send(slot).start()

    @pl.loop(0, P_MAX)
    def _(slot):
        @pl.when(is_in(wanted[slot], distances))
        def _():
            send(slot).wait()


def tiles(distances, wanted, stacked, own, other, so_far, by_slot=False):
    rows = stacked.shape
    half = rows[0] // PAIRS
    count = 2 * half
    stacked = pltpu.with_memory_space_constraint(stacked, pltpu.VMEM)
    arguments = [wanted, stacked, *own, *other, so_far]
    return pl.pallas_call(
        functools.partial(tile_kernel, distances, by_slot),
        out_shape=jax.ShapeDtypeStruct(so_far.shape, so_far.dtype),
        in_specs=[SMEM] + [VMEM] * (len(arguments) - 2) + [ANY],
        out_specs=ANY,
        scratch_shapes=[
            pltpu.VMEM((2 * count, rows[1]), jnp.bfloat16),
            pltpu.VMEM((P_MAX, LAGS, half, count), jnp.float32),
            pltpu.SemaphoreType.DMA((P_MAX,)),
        ],
        input_output_aliases={len(arguments) - 1: 0},
        compiler_params=pltpu.CompilerParams(vmem_limit_bytes=16 * 2**20),
        cost_estimate=FREE,
        name="tiles_" + "_".join(map(str, distances)),
    )(*arguments)


def body(traces, pair_target, pair_count):
    own = traces[0, 0]
    half = own.shape[0] // 2
    blocks = lax.axis_size("chan")
    me, core = lax.axis_index("chan"), lax.axis_index("tm")
    slots = jnp.arange(P_MAX, dtype=jnp.int32)
    wanted = jnp.where(slots < pair_count[0], pair_target[0] - me, 0).astype(jnp.int32)

    row = 8
    everyone = range(blocks)
    down = [((i + 1) % blocks, i) for i in everyone]
    up = [((i - 1) % blocks, i) for i in everyone]
    next_row = [((i + row) % blocks, i) if i % row < row - 1 else (i, i) for i in everyone]
    turn = [(i - 1, i) if i % row else (i + row - 1, i) for i in everyone]

    def move(parts, route):
        return [lax.ppermute(p, "chan", route) for p in parts]

    def swap(parts):
        return [lax.ppermute(p, "tm", [(0, 1), (1, 0)]) for p in parts]

    def step(*values):
        return lax.optimization_barrier(values)

    mine = lax.dynamic_slice_in_dim(own, core * half, half, 0)
    theirs = lax.dynamic_slice_in_dim(own, (1 - core) * half, half, 0)
    d1 = move([own], down)[0]
    below = move([own], next_row)[0]
    before = move([own], turn)[0]
    theirs = swap([theirs])[0]
    below, before, theirs, d1 = step(below, before, theirs, d1)
    d7 = move([below], turn)[0]
    d2 = move([d1], down[:-1])[0]
    rows, result = stack(wanted, mine, theirs)
    d7, rows, result = step(d7, rows, result)
    d6 = move([jnp.where(me % row == row - 1, before, d7)], turn)[0]
    d3 = move([d2], down)[0]
    d5 = move([d6], up)[0]
    d4 = move([d3], down)[0]
    near = pick((1, 7, 2, 6), wanted, [d1, d7, d2, d6])
    result = tiles((1, 7, 2, 6), wanted, rows, near, swap(near), result, True)
    d5, result = step(d5, result)
    return tiles((3, 5, 4), wanted, rows, [d3, d5, d4], swap([d3, d5, d4]), result)


def solution(mesh):
    placed = (P("tm", "chan", None, None), P("chan", None), P("chan"))
    return jax.shard_map(
        body,
        mesh=mesh,
        in_specs=placed,
        out_specs=P("chan", None, None, "tm", None),
        check_vma=False,
    )
```
